256 devices in a mesh: leaf: 32 (over z, y), sub: 8 (over x, core).
Axes of the slice: x: 4, y: 4, z: 8, core: 2. Of those that a mesh axis runs over, the one named last changes fastest.
Arguments:
- bottom_coeffs: bfloat16 [8192, 64, 64], P(('leaf', 'sub')), may hold values from -6 to 6
- local_transfer: bfloat16 [256, 63, 64, 64], P(('leaf', 'sub')), may hold values from -0.5 to 0.5
- coarse_transfer: bfloat16 [32, 6, 64, 64], P('leaf'), may hold values from -0.5 to 0.5
- local_coupling: bfloat16 [256, 63, 16, 64, 64], P(('leaf', 'sub')), may hold values from -0.1875 to 0.1875
- local_partners: int32 [256, 63, 16], P(('leaf', 'sub')), may hold values from -32 to 32, as said below
- local_counts: int32 [256, 63], P(('leaf', 'sub')), may hold values from 1 to 16
- coarse_coupling: bfloat16 [32, 7, 16, 64, 64], P('leaf'), may hold values from -0.1875 to 0.1875
- coarse_partners: int32 [32, 7, 16], P('leaf'), may hold values from 0 to 127, as said below
- coarse_counts: int32 [32, 7], P('leaf'), may hold values from 1 to 16
Outputs:
- far_field: bfloat16 [8192, 64, 64], P(('leaf', 'sub'))
The draws below stay inside these ranges and needn't reach their ends.
Inputs may be any that keep to these rules, and one draw needn't show every extreme that they name: `local_partners`: A cluster at a level with n clusters a device has offsets from -n to n. `coarse_partners`: A partner of a coarse node at depth t lies in the level with 32 * 2^t clusters.
All inputs are finite; a program needn't handle non-finite values.
Results may differ from the reference program's by a relative error of at most 0.023.
Values may be sent and summed in bfloat16 or wider, within the bound.
A program may use at most 128 MiB of HBM per device.

```python
import jax
import jax.numpy as jnp
import numpy as np

R = 64
Q = 64
K = 16
C_DEV = 32
BOTTOM = 8192
SLOTS = 63
NODES = 7
LIFTS = 6
N_LEAF = 32
N_SUB = 8
DEVICES = 256


def heap_spans(count):
    return np.array([1 << int(s).bit_length() - 1 for s in range(1, count + 1)], dtype=np.int32)


def draw_local_partners(key, part):
    key = jax.random.fold_in(key, 11)
    spans = jnp.asarray(heap_spans(2 * C_DEV - 1))[None, :, None]
    drawn = jax.random.randint(key, (DEVICES, 2 * C_DEV - 1, K), -spans, spans + 1, dtype=jnp.int32)
    drawn = drawn.at[:, C_DEV - 1, 0].set(-C_DEV)
    return drawn.at[:, C_DEV - 1, 1].set(C_DEV)


def draw_local_counts(key, part):
    key = jax.random.fold_in(key, 12)
    drawn = jax.random.randint(key, (DEVICES, 2 * C_DEV - 1), 1, K + 1, dtype=jnp.int32)
    drawn = drawn.at[:, C_DEV - 1].set(K)
    return drawn.at[:, C_DEV].set(1)


def draw_coarse_partners(key, part):
    key = jax.random.fold_in(key, 13)
    spans = jnp.asarray(heap_spans(N_SUB - 1))[None, :, None] * N_LEAF
    drawn = jax.random.randint(key, (N_LEAF, N_SUB - 1, K), 0, spans, dtype=jnp.int32)
    return drawn.at[0, N_SUB - 2, 0].set(N_LEAF * N_SUB // 2 - 1)


def draw_coarse_counts(key, part):
    key = jax.random.fold_in(key, 14)
    drawn = jax.random.randint(key, (N_LEAF, N_SUB - 1), 1, K + 1, dtype=jnp.int32)
    drawn = drawn.at[:, 0].set(K)
    return drawn.at[:, 1].set(1)


def level_of(rng, extent, pieces, least, top_value):
    level, own = 1.0, jax.random.fold_in(rng, 6)
    for axis_at, parts in pieces:
        heights = jnp.exp(jax.random.uniform(jax.random.fold_in(own, axis_at), (parts,), jnp.float32, least / len(pieces), top_value / len(pieces)))
        level = level * jnp.repeat(heights, extent[axis_at] // parts).reshape([-1 if axis == axis_at else 1 for axis in range(len(extent))])
    return level


def centred(rng, dims, deviation, most, pieces=(), kind=jnp.bfloat16):
    loudness = level_of(rng, dims, pieces, -0.22, 0.18) if pieces else 1.0
    result = jax.random.normal(rng, dims, jnp.float32) * deviation * loudness
    return jnp.minimum(jnp.maximum(result, -most), most).astype(kind)


def setup_inputs(seed: int = 0) -> dict:
    streams_of = jax.random.split(jax.random.key(seed), 10)
    return {
        "bottom_coeffs": centred(streams_of[0], (BOTTOM, R, Q), 1.0, 6.0, ((0, 256),)),
        "local_transfer": centred(streams_of[1], (DEVICES, SLOTS, R, R), (2 * R) ** -0.5, 0.5, ((0, 256),)),
        "coarse_transfer": centred(streams_of[2], (N_LEAF, LIFTS, R, R), (2 * R) ** -0.5, 0.5, ((0, 32),)),
        "local_coupling": centred(streams_of[3], (DEVICES, SLOTS, K, R, R), (K * R) ** -0.5, 0.1875, ((0, 256),)),
        "local_partners": draw_local_partners(jax.random.fold_in(streams_of[9], 71), 0),
        "local_counts": draw_local_counts(jax.random.fold_in(streams_of[9], 71), 0),
        "coarse_coupling": centred(streams_of[6], (N_LEAF, NODES, K, R, R), (K * R) ** -0.5, 0.1875, ((0, 32),)),
        "coarse_partners": draw_coarse_partners(jax.random.fold_in(streams_of[9], 71), 0),
        "coarse_counts": draw_coarse_counts(jax.random.fold_in(streams_of[9], 71), 0),
    }


def unpack_level(packed, first, count):
    section = packed[:, first:first + count]
    return section.reshape((section.shape[0] * count,) + section.shape[2:])


def lift_level(child_coeffs, child_transfer):
    products = jnp.einsum('iab,ibq->iaq', child_transfer.astype(jnp.float32), child_coeffs.astype(jnp.float32))
    paired = products.reshape((products.shape[0] // 2, 2) + products.shape[1:])
    return (paired[:, 0] + paired[:, 1]).astype(jnp.bfloat16)


def couple_level(source, where_from, counts, blocks):
    summed = jnp.zeros((where_from.shape[0], blocks.shape[2], source.shape[2]), jnp.float32)
    for slot in range(where_from.shape[1]):
        active = (counts > slot).astype(jnp.float32)
        chosen = source[where_from[:, slot]].astype(jnp.float32) * active[:, None, None]
        summed = summed + jnp.einsum('iab,ibq->iaq', blocks[:, slot].astype(jnp.float32), chosen)
    return summed


def lower_level(coupled, spread, transfer):
    return (coupled + jnp.einsum('iba,ibq->iaq', transfer.astype(jnp.float32), spread.astype(jnp.float32))).astype(jnp.bfloat16)


def reference(bottom_coeffs, local_transfer, coarse_transfer, local_coupling, local_partners, local_counts, coarse_coupling, coarse_partners, coarse_counts):
    widths = []
    n = C_DEV
    while n >= 1:
        widths.append(n)
        n = n // 2
    coeffs = {C_DEV: bottom_coeffs}
    for n in widths[1:]:
        coeffs[n] = lift_level(coeffs[2 * n], unpack_level(local_transfer, 2 * n - 1, 2 * n))
    coupled = {}
    for n in widths:
        offsets = unpack_level(local_partners, n - 1, n)
        position = jnp.arange(offsets.shape[0], dtype=jnp.int32)[:, None] + n
        padded = jnp.pad(coeffs[n], ((n, n), (0, 0), (0, 0)))
        coupled[n] = couple_level(padded, (position + offsets).astype(jnp.int32), unpack_level(local_counts, n - 1, n), unpack_level(local_coupling, n - 1, n))
    tree_depth = N_SUB.bit_length() - 1
    upper = {}
    children = coeffs[1]
    child_transfer = unpack_level(local_transfer, 0, 1)
    for t in range(tree_depth - 1, -1, -1):
        upper[t] = lift_level(children, child_transfer)
        children = upper[t]
        if t > 0:
            child_transfer = unpack_level(coarse_transfer, 2 ** t - 2, 2 ** t)
    coarse_sums = {}
    for t in range(tree_depth):
        span = 2 ** t
        coarse_sums[t] = couple_level(upper[t], unpack_level(coarse_partners, span - 1, span), unpack_level(coarse_counts, span - 1, span), unpack_level(coarse_coupling, span - 1, span))
    values = coarse_sums[0].astype(jnp.bfloat16)
    for t in range(1, tree_depth):
        values = lower_level(coarse_sums[t], jnp.repeat(values, 2, axis=0), unpack_level(coarse_transfer, 2 ** t - 2, 2 ** t))
    values = lower_level(coupled[1], jnp.repeat(values, 2, axis=0), unpack_level(local_transfer, 0, 1))
    for n in widths[-2::-1]:
        values = lower_level(coupled[n], jnp.repeat(values, 2, axis=0), unpack_level(local_transfer, n - 1, n))
    return values
```

```python
import jax
import jax.numpy as jnp
from jax import lax
from jax.experimental import pallas as pl
from jax.experimental.pallas import tpu as pltpu
from jax.sharding import PartitionSpec as P

F32 = jnp.float32
BF16 = jnp.bfloat16
MESH = pl.DeviceIdType.MESH

R = 64
K = 16
C = 32
UP = C - 1
SLOTS = 2 * C - 1
LEAF = 32
SUB = 8
NZ, NY = 8, 4
DEVICES = LEAF * SUB
ZERO_B = 3 * C
ZERO_U = 3 * UP
ZERO_P = LEAF * 8
NT = (((1,), (1,)), ((), ()))


def mm(a, b):
    return jnp.dot(a, b, preferred_element_type=F32)


def mm_nt(a, b):
    return lax.dot_general(a, b, NT, preferred_element_type=F32)


def fold(block):
    return jnp.concatenate([block[: R // 2], block[R // 2 :]], axis=1)


def couple(index, first, slot, blocks, source):
    total = jnp.zeros((R, R), F32)
    for k0 in range(0, K, 4):
        left = jnp.concatenate([blocks[slot, k] for k in range(k0, k0 + 4)], axis=1)
        right = jnp.concatenate([source[index[k, slot]] for k in range(k0, k0 + 4)], axis=0)
        total = total + mm(left, right)
    return total


def kernel(
    bottom, transfer, coarse_transfer, coupling, coarse_coupling, partners, counts, coarse_partners, coarse_counts,
    out,
    xb, xu, f, cf, s, cs, cscat, ft, g, w, zb, zu,
    send_b, send_u, recv_b, recv_u, pt, r, mine, pool, poolf, ys, yr, outv,
    part_v, count_v, index_v, index_s, cpart_s, ccount_s, cindex_s,
    load_sem, small_sem, out_sem, halo_s, halo_r, lift_s, lift_r, z_s, z_r, y_s, y_r, low_s, low_r,
):
    leaf = lax.axis_index("leaf")
    sub = lax.axis_index("sub")
    me = leaf * SUB + sub
    at_z = lax.div(leaf, NY)
    at_y = lax.rem(leaf, NY)
    after = lax.rem(me + 1, DEVICES)
    before = lax.rem(me + DEVICES - 1, DEVICES)
    sides = [(lax.div(d, SUB), lax.rem(d, SUB)) for d in (before, after)]
    group = [lax.rem(sub + i, SUB) for i in range(1, SUB)]
    along_z = [lax.rem(at_z + i, NZ) * NY + at_y for i in range(1, NZ)]
    along_y = [at_z * NY + lax.rem(at_y + i, NY) for i in range(1, NY)]

    load = lambda a, b, i: pltpu.make_async_copy(a, b, load_sem.at[i])
    get_x = load(bottom, xb.at[pl.ds(C, C)], 0)
    get_fb = load(transfer.at[pl.ds(UP, C)], f.at[pl.ds(UP, C)], 1)
    get_fu = load(transfer.at[pl.ds(0, UP)], f.at[pl.ds(0, UP)], 2)
    get_cf = load(coarse_transfer, cf, 3)
    get_cs = load(coarse_coupling, cs, 4)
    get_su = load(coupling.at[pl.ds(0, UP)], s.at[pl.ds(0, UP)], 5)
    get_sb = load(coupling.at[pl.ds(UP, C)], s.at[pl.ds(UP, C)], 6)
    small = lambda a, b, i: pltpu.make_async_copy(a, b, small_sem.at[i])
    get_part = small(partners, part_v, 0)
    get_count = small(counts, count_v, 1)
    get_cpart = small(coarse_partners, cpart_s, 2)
    get_ccount = small(coarse_counts, ccount_s, 3)
    for copy in (get_x, get_fb, get_fu, get_part, get_count, get_cf, get_cpart, get_ccount):
        copy.start()

    barrier = pltpu.get_barrier_semaphore()
    for peer in sides:
        pl.semaphore_signal(barrier, inc=1, device_id=peer, device_id_type=MESH)
    for peer in group:
        pl.semaphore_signal(barrier, inc=1, device_id=(leaf, peer), device_id_type=MESH)
    for peer in along_z + along_y:
        pl.semaphore_signal(barrier, inc=1, device_id=(peer, sub), device_id_type=MESH)

    xb[ZERO_B] = jnp.zeros((R, R), BF16)
    xu[ZERO_U] = jnp.zeros((R, R), BF16)
    poolf[ZERO_P] = jnp.zeros((8, R), F32)

    get_x.wait()
    for i in range(C):
        send_b[i] = fold(xb[C + i])
    get_su.start()
    pl.semaphore_wait(barrier, 2 + (SUB - 1) + (NZ - 1) + (NY - 1))

    def remote(src, dst, ss, rs, peer):
        return pltpu.make_async_remote_copy(
            src_ref=src, dst_ref=dst, send_sem=ss, recv_sem=rs, device_id=peer, device_id_type=MESH
        )

    halo_b = [remote(send_b, recv_b.at[1 - i], halo_s.at[i], halo_r.at[i], sides[i]) for i in range(2)]
    halo_u = [remote(send_u, recv_u.at[1 - i], halo_s.at[2 + i], halo_r.at[2 + i], sides[i]) for i in range(2)]
    for copy in halo_b:
        copy.start()

    get_fb.wait()
    get_fu.wait()
    n = C // 2
    while n >= 1:
        for i in range(n):
            a = 2 * (n + i) - 1
            left = jnp.concatenate([f[a], f[a + 1]], axis=1)
            right = (xb[pl.ds(C + 2 * i, 2)] if n == C // 2 else xu[pl.ds(UP + a, 2)]).reshape(2 * R, R)
            xu[UP + n + i - 1] = mm(left, right).astype(BF16)
        n //= 2
    lifted = jnp.transpose(mm(f[0], xu[UP]))
    pt[...] = lifted.reshape(SUB, 8, R)
    lifts = [
        remote(pt.at[peer], r.at[sub], lift_s.at[i], lift_r.at[i], (leaf, peer)) for i, peer in enumerate(group)
    ]
    for copy in lifts:
        copy.start()
    r[pl.ds(sub, 1)] = pt[pl.ds(sub, 1)]

    for i in range(UP):
        send_u[i] = fold(xu[UP + i])
    for copy in halo_u:
        copy.start()
    get_sb.start()
    get_cs.start()

    get_part.wait()
    get_count.wait()
    node = lax.broadcasted_iota(jnp.int32, (K, SLOTS), 1) + 1
    step = lax.broadcasted_iota(jnp.int32, (K, SLOTS), 0)
    width = jnp.ones((K, SLOTS), jnp.int32)
    for t in range(1, 6):
        width = jnp.where(node >= 2**t, 2**t, width)
    target = node - width + part_v[...]
    window = jnp.where(target < 0, 0, jnp.where(target < width, 1, 2))
    where_u = window * UP + (width - 1) + target + width - window * width
    is_bottom = node >= C
    where_from = jnp.where(is_bottom, C + target, where_u)
    ended = step >= jnp.broadcast_to(count_v[...], (K, SLOTS))
    where_from = jnp.where(ended, jnp.where(is_bottom, ZERO_B, ZERO_U), where_from)
    index_v[:, pl.ds(0, SLOTS)] = where_from
    to_smem = small(index_v, index_s, 4)
    to_smem.start()

    g[0] = jnp.transpose(f[0])
    for h in range(1, C):
        ft[h - 1] = jnp.transpose(jnp.concatenate([f[2 * h - 1], f[2 * h]], axis=1))
    for h in range(1, C):
        g[pl.ds(2 * h - 1, 2)] = mm(ft[h - 1], g[h - 1]).astype(BF16).reshape(2, R, R)

    get_cf.wait()
    for copy in lifts:
        copy.wait_recv()
    rounded = lambda a: a.astype(BF16).astype(F32)
    x2 = [rounded(r[2 * j] + r[2 * j + 1]) for j in range(4)]
    pair_a = jnp.concatenate([x2[0], x2[1]], axis=1)
    pair_b = jnp.concatenate([x2[2], x2[3]], axis=1)
    none = jnp.zeros((8, 2 * R), F32)
    left = jnp.concatenate(
        [jnp.concatenate([pair_a, none], axis=1), jnp.concatenate([none, pair_b], axis=1)], axis=0
    ).astype(BF16)
    x1 = rounded(mm_nt(left, jnp.concatenate([cf[2 + j] for j in range(4)], axis=1)))
    pair_c = jnp.concatenate([x1[:8], x1[8:]], axis=1)
    x0 = mm_nt(pair_c.astype(BF16), jnp.concatenate([cf[0], cf[1]], axis=1))
    pair_d = jnp.concatenate([x0, jnp.zeros((8, R), F32)], axis=1)
    mine[...] = jnp.concatenate([pair_a, pair_b, pair_c, pair_d], axis=0).astype(BF16)
    over_z = [
        remote(mine, pool.at[at_y, at_z], z_s.at[i], z_r.at[i], (peer, sub)) for i, peer in enumerate(along_z)
    ]
    for copy in over_z:
        copy.start()
    pool[pl.ds(at_y, 1), pl.ds(at_z, 1)] = mine[...].reshape(1, 1, 32, 2 * R)

    get_cpart.wait()
    get_ccount.wait()
    for t in range(3):
        for j in range(2**t):
            i = 2**t - 1 + j
            for k in range(K):
                p = cpart_s[i, 0, k]
                its = lax.shift_right_logical(p, t)
                inside = p - lax.shift_left(its, t)
                place = lax.rem(its, NY) * NZ + lax.div(its, NY)
                place = place * 8 + (0, 4, 6)[2 - t] + inside
                cindex_s[i * K + k] = jnp.where(k < ccount_s[0, i], place, ZERO_P)
    get_cs.wait()
    for i in range(7):
        for k0 in range(0, K, 4):
            cscat[i, :, pl.ds(k0 * R, 4 * R)] = jnp.concatenate([cs[i, k] for k in range(k0, k0 + 4)], axis=1)

    for copy in over_z:
        copy.wait_recv()
    over_y = [
        remote(pool.at[at_y], pool.at[at_y], y_s.at[i], y_r.at[i], (peer, sub)) for i, peer in enumerate(along_y)
    ]
    for copy in over_y:
        copy.start()

    for copy in halo_b + halo_u:
        copy.wait_recv()
    to_smem.wait()
    for side in range(2):
        for i in range(UP):
            v = recv_u[side, i]
            xu[2 * UP * side + i] = jnp.concatenate([v[:, :R], v[:, R:]], axis=0)
        for i in range(C):
            v = recv_b[side, i]
            xb[2 * C * side + i] = jnp.concatenate([v[:, :R], v[:, R:]], axis=0)
    for side, end in ((0, 0), (1, DEVICES - 1)):

        @pl.when(me == end)
        def _():
            xu[pl.ds(2 * UP * side, UP)] = jnp.zeros((UP, R, R), BF16)
            xb[pl.ds(2 * C * side, C)] = jnp.zeros((C, R, R), BF16)

    get_su.wait()

    @pl.loop(0, UP, unroll=UP)
    def _(i):
        zu[i] = couple(index_s, 0, i, s, xu)

    w[0] = zu[0].astype(BF16)
    for h in range(1, C // 2):
        low = zu[pl.ds(2 * h - 1, 2)].reshape(2 * R, R) + mm(ft[h - 1], w[h - 1])
        w[pl.ds(2 * h - 1, 2)] = low.astype(BF16).reshape(2, R, R)

    for copy in over_y:
        copy.wait_recv()
    for y in range(NY):
        for z in range(NZ):
            v = pool[y, z].astype(F32)
            for b in range(4):
                poolf[(y * NZ + z) * 8 + 2 * b] = v[8 * b : 8 * b + 8, :R]
                poolf[(y * NZ + z) * 8 + 2 * b + 1] = v[8 * b : 8 * b + 8, R:]
    zc = []
    for i in range(7):
        left = jnp.concatenate([poolf[cindex_s[i * K + k]] for k in range(K)], axis=1)
        zc.append(mm_nt(left.astype(BF16), cscat[i]))
    y1 = jnp.concatenate([zc[1], zc[2]], axis=1) + mm(
        zc[0].astype(BF16), jnp.concatenate([cf[0], cf[1]], axis=1)
    )
    y1 = y1.astype(BF16)
    y2a = jnp.concatenate([zc[3], zc[4]], axis=1) + mm(y1[:, :R], jnp.concatenate([cf[2], cf[3]], axis=1))
    y2b = jnp.concatenate([zc[5], zc[6]], axis=1) + mm(y1[:, R:], jnp.concatenate([cf[4], cf[5]], axis=1))
    for j, v in enumerate((y2a, y2b)):
        v = rounded(v)
        ys[2 * j] = v[:, :R]
        ys[2 * j + 1] = v[:, R:]
    lows = [
        remote(ys.at[lax.div(peer, 2)], yr.at[sub], low_s.at[i], low_r.at[i], (leaf, peer))
        for i, peer in enumerate(group)
    ]
    for copy in lows:
        copy.start()
    yr[pl.ds(sub, 1)] = ys[pl.ds(lax.div(sub, 2), 1)]

    get_sb.wait()

    @pl.loop(0, C, unroll=C)
    def _(i):
        zb[i] = couple(index_s, 0, UP + i, s, xb)

    for i in range(C // 2):
        h = C // 2 + i
        low = zb[pl.ds(2 * i, 2)].reshape(2 * R, R) + mm(ft[h - 1], w[h - 1])
        zb[pl.ds(2 * i, 2)] = low.reshape(2, R, R)

    for copy in lows:
        copy.wait_recv()
    yp = yr[...].reshape(R, R).astype(BF16)
    puts = []
    part = C // 4
    for c in range(4):
        far = mm_nt(g[pl.ds(UP + c * part, part)].reshape(part * R, R), yp).reshape(part, R, R)
        outv[pl.ds(c * part, part)] = (zb[pl.ds(c * part, part)] + far).astype(BF16)
        put = pltpu.make_async_copy(
            outv.at[pl.ds(c * part, part)], out.at[pl.ds(c * part, part)], out_sem.at[c]
        )
        put.start()
        puts.append(put)
    for copy in halo_b + halo_u + lifts + over_z + over_y + lows:
        copy.wait_send()
    for put in puts:
        put.wait()


def on_device(
    bottom, transfer, coarse_transfer, coupling, partners, counts, coarse_coupling, coarse_partners, coarse_counts
):
    dma = pltpu.SemaphoreType.DMA
    any_space = pl.BlockSpec(memory_space=pl.ANY)
    return pl.pallas_call(
        kernel,
        out_shape=jax.ShapeDtypeStruct((C, R, R), BF16),
        in_specs=[any_space] * 9,
        out_specs=any_space,
        scratch_shapes=[
            pltpu.VMEM((3 * C + 1, R, R), BF16),
            pltpu.VMEM((3 * UP + 1, R, R), BF16),
            pltpu.VMEM((SLOTS, R, R), BF16),
            pltpu.VMEM((6, R, R), BF16),
            pltpu.VMEM((SLOTS, K, R, R), BF16),
            pltpu.VMEM((7, K, R, R), BF16),
            pltpu.VMEM((7, R, K * R), BF16),
            pltpu.VMEM((UP, 2 * R, R), BF16),
            pltpu.VMEM((SLOTS, R, R), BF16),
            pltpu.VMEM((UP, R, R), BF16),
            pltpu.VMEM((C, R, R), F32),
            pltpu.VMEM((UP, R, R), F32),
            pltpu.VMEM((C, R // 2, 2 * R), BF16),
            pltpu.VMEM((UP, R // 2, 2 * R), BF16),
            pltpu.VMEM((2, C, R // 2, 2 * R), BF16),
            pltpu.VMEM((2, UP, R // 2, 2 * R), BF16),
            pltpu.VMEM((SUB, 8, R), F32),
            pltpu.VMEM((SUB, 8, R), F32),
            pltpu.VMEM((32, 2 * R), BF16),
            pltpu.VMEM((NY, NZ, 32, 2 * R), BF16),
            pltpu.VMEM((LEAF * 8 + 1, 8, R), F32),
            pltpu.VMEM((4, 8, R), F32),
            pltpu.VMEM((SUB, 8, R), F32),
            pltpu.VMEM((C, R, R), BF16),
            pltpu.VMEM((K, SLOTS), jnp.int32),
            pltpu.VMEM((1, SLOTS), jnp.int32),
            pltpu.VMEM((K, 128), jnp.int32),
            pltpu.SMEM((K, 128), jnp.int32),
            pltpu.SMEM((7, 1, K), jnp.int32),
            pltpu.SMEM((1, 7), jnp.int32),
            pltpu.SMEM((7 * K,), jnp.int32),
            dma((7,)), dma((5,)), dma((4,)),
            dma((4,)), dma((4,)), dma((7,)), dma((7,)), dma((7,)), dma((7,)),
            dma((3,)), dma((3,)), dma((7,)), dma((7,)),
        ],
        compiler_params=pltpu.CompilerParams(
            collective_id=0, has_side_effects=True, vmem_limit_bytes=56 * 2**20
        ),
        cost_estimate=pl.CostEstimate(flops=700_000_000, bytes_accessed=21_000_000, transcendentals=0),
    )(
        bottom,
        transfer.reshape(SLOTS, R, R),
        coarse_transfer.reshape(6, R, R),
        coupling.reshape(SLOTS, K, R, R),
        coarse_coupling.reshape(7, K, R, R),
        jnp.transpose(partners, (0, 2, 1)).reshape(K, SLOTS),
        counts,
        jnp.transpose(coarse_partners, (1, 0, 2)),
        coarse_counts,
    )


def solution(mesh):
    wide = P(("leaf", "sub"))
    placed = (wide, wide, P("leaf"), wide, wide, wide, P("leaf"), P("leaf"), P("leaf"))
    return jax.shard_map(on_device, mesh=mesh, in_specs=placed, out_specs=wide, check_vma=False)
```

```python
import jax
import jax.numpy as jnp
from jax import lax
from jax.experimental import pallas as pl
from jax.experimental.pallas import tpu as pltpu
from jax.sharding import PartitionSpec as P

F32 = jnp.float32
BF16 = jnp.bfloat16
MESH = pl.DeviceIdType.MESH

R = 64
K = 16
C = 32
UP = C - 1
SLOTS = 2 * C - 1
LEAF = 32
SUB = 8
NZ, NY = 8, 4
DEVICES = LEAF * SUB
ZERO_B = 3 * C
ZERO_U = 3 * UP
ZERO_P = 3 * LEAF
H = R // 2
NT = (((1,), (1,)), ((), ()))


def mm(a, b):
    return jnp.dot(a, b, preferred_element_type=F32)


def mm_nt(a, b):
    return lax.dot_general(a, b, NT, preferred_element_type=F32)


def fold(block):
    half = block.shape[0] // 2
    return jnp.concatenate([block[:half], block[half:]], axis=1)


def unfold(block):
    return jnp.concatenate([block[:, :R], block[:, R:]], axis=0)


def couple(index, first, slot, blocks, source):
    total = jnp.zeros((R, R), F32)
    for k0 in range(0, K, 4):
        left = jnp.concatenate([blocks[slot, k] for k in range(k0, k0 + 4)], axis=1)
        right = jnp.concatenate([source[index[k, slot]] for k in range(k0, k0 + 4)], axis=0)
        total = total + mm(left, right)
    return total


def kernel(
    bottom, transfer, coarse_transfer, coupling, coarse_coupling, partners, counts, coarse_partners, coarse_counts,
    out,
    xb, xu, f, cf, s, cs, cscat, ft, g, w, zb, zu,
    send_b, send_u, recv_b, recv_u, pt, pr, lift, mine, pool, xc, ys, yr,
    part_v, count_v, index_v, index_s, cpart_s, ccount_s, cindex_s,
    load_sem, small_sem, halo_s, halo_r, core_s, core_r, z_s, z_r, y_s, y_r, low_s, low_r,
):
    leaf = lax.axis_index("leaf")
    sub = lax.axis_index("sub")
    me = leaf * SUB + sub
    at_z = lax.div(leaf, NY)
    at_y = lax.rem(leaf, NY)
    chip = lax.div(sub, 2)
    core = lax.rem(sub, 2)
    after = lax.rem(me + 1, DEVICES)
    before = lax.rem(me + DEVICES - 1, DEVICES)
    sides = [(lax.div(d, SUB), lax.rem(d, SUB)) for d in (before, after)]
    group = [lax.rem(sub + i, SUB) for i in range(1, SUB)]
    along_z = [lax.rem(at_z + i, NZ) * NY + at_y for i in range(1, NZ)]
    along_y = [at_z * NY + lax.rem(at_y + i, NY) for i in range(1, NY)]

    load = lambda a, b, i: pltpu.make_async_copy(a, b, load_sem.at[i])
    get_x = load(bottom, xb.at[pl.ds(C, C)], 0)
    get_fb = load(transfer.at[pl.ds(UP, C)], f.at[pl.ds(UP, C)], 1)
    get_fu = load(transfer.at[pl.ds(0, UP)], f.at[pl.ds(0, UP)], 2)
    get_cf = load(coarse_transfer, cf, 3)
    get_cs = load(coarse_coupling, cs, 4)
    get_su = load(coupling.at[pl.ds(0, UP)], s.at[pl.ds(0, UP)], 5)
    get_sb = load(coupling.at[pl.ds(UP, C)], s.at[pl.ds(UP, C)], 6)
    small = lambda a, b, i: pltpu.make_async_copy(a, b, small_sem.at[i])
    get_part = small(partners, part_v, 0)
    get_count = small(counts, count_v, 1)
    get_cpart = small(coarse_partners, cpart_s, 2)
    get_ccount = small(coarse_counts, ccount_s, 3)
    for copy in (get_x, get_fb, get_fu, get_cf):
        copy.start()
    barrier = pltpu.get_barrier_semaphore()
    for peer in along_z + along_y:
        pl.semaphore_signal(barrier, inc=1, device_id=(peer, sub), device_id_type=MESH)
    for peer in sides:
        pl.semaphore_signal(barrier, inc=1, device_id=peer, device_id_type=MESH)
    for peer in group:
        pl.semaphore_signal(barrier, inc=1, device_id=(leaf, peer), device_id_type=MESH)

    for copy in (get_part, get_count, get_cpart, get_ccount):
        copy.start()
    xb[ZERO_B] = jnp.zeros((R, R), BF16)
    xu[ZERO_U] = jnp.zeros((R, R), BF16)
    xc[ZERO_P] = jnp.zeros((H, R), BF16)

    get_x.wait()
    get_fb.wait()
    get_fu.wait()
    n = C // 2
    while n >= 1:
        for i in range(n):
            a = 2 * (n + i) - 1
            left = jnp.concatenate([f[a], f[a + 1]], axis=1)
            right = (xb[pl.ds(C + 2 * i, 2)] if n == C // 2 else xu[pl.ds(UP + a, 2)]).reshape(2 * R, R)
            xu[UP + n + i - 1] = mm(left, right).astype(BF16)
        n //= 2
    pt[...] = jnp.transpose(mm(f[0], xu[UP])).reshape(2, H, R)

    get_cf.wait()
    ones = lax.broadcasted_iota(jnp.int32, (R, R), 0) == lax.broadcasted_iota(jnp.int32, (R, R), 1)
    lift[pl.ds(0, R)] = ones.astype(F32).astype(BF16)
    lift[pl.ds(R, R)] = cf[2 + chip]
    lift[pl.ds(2 * R, R)] = mm(cf[lax.div(chip, 2)], cf[2 + chip]).astype(BF16)
    for i in range(C):
        send_b[i] = fold(xb[C + i])

    pl.semaphore_wait(barrier, 2 + (SUB - 1) + (NZ - 1) + (NY - 1))

    def remote(src, dst, ss, rs, peer):
        return pltpu.make_async_remote_copy(
            src_ref=src, dst_ref=dst, send_sem=ss, recv_sem=rs, device_id=peer, device_id_type=MESH
        )

    swap = remote(pt.at[1 - core], pr, core_s.at[0], core_r.at[0], (leaf, chip * 2 + 1 - core))
    swap.start()
    get_cs.start()

    halo_b = [remote(send_b, recv_b.at[1 - i], halo_s.at[i], halo_r.at[i], sides[i]) for i in range(2)]
    halo_u = [remote(send_u, recv_u.at[1 - i], halo_s.at[2 + i], halo_r.at[2 + i], sides[i]) for i in range(2)]
    for copy in halo_b:
        copy.start()

    swap.wait_recv()
    node = (pt[pl.ds(core, 1)].reshape(H, R) + pr[...]).astype(BF16)
    piece = mm_nt(node, lift[...])
    mine[pl.ds(0, H)] = piece[:, : 2 * R].astype(BF16)
    mine[pl.ds(H, H // 2)] = fold(piece[:, 2 * R :]).astype(BF16)
    over_z = [
        remote(mine, pool.at[at_y, at_z], z_s.at[i], z_r.at[i], (peer, sub)) for i, peer in enumerate(along_z)
    ]
    over_y = [
        [
            remote(
                mine if i == NZ - 1 else pool.at[at_y, from_z],
                pool.at[at_y, from_z],
                y_s.at[i, m],
                y_r.at[i, m],
                (peer, sub),
            )
            for m, peer in ((1, along_y[1]), (0, along_y[0]), (2, along_y[2]))
        ]
        for i, from_z in enumerate([lax.rem(at_z + NZ - 1 - i, NZ) for i in range(NZ)])
    ]
    for i in (0, 6, 1, 5, 2, 4, 3):
        over_z[i].start()
    for copy in over_y[NZ - 1]:
        copy.start()
    get_sb.start()
    pool[pl.ds(at_y, 1), pl.ds(at_z, 1)] = mine[...].reshape(1, 1, 3 * H // 2, 2 * R)

    for i in range(UP):
        send_u[i] = fold(xu[UP + i])
    for copy in halo_u:
        copy.start()

    get_part.wait()
    get_count.wait()
    node = lax.broadcasted_iota(jnp.int32, (K, SLOTS), 1) + 1
    step = lax.broadcasted_iota(jnp.int32, (K, SLOTS), 0)
    width = jnp.ones((K, SLOTS), jnp.int32)
    for t in range(1, 6):
        width = jnp.where(node >= 2**t, 2**t, width)
    target = node - width + part_v[...]
    window = jnp.where(target < 0, 0, jnp.where(target < width, 1, 2))
    where_u = window * UP + (width - 1) + target + width - window * width
    is_bottom = node >= C
    where_from = jnp.where(is_bottom, C + target, where_u)
    ended = step >= jnp.broadcast_to(count_v[...], (K, SLOTS))
    where_from = jnp.where(ended, jnp.where(is_bottom, ZERO_B, ZERO_U), where_from)
    index_v[:, pl.ds(0, SLOTS)] = where_from
    to_smem = small(index_v, index_s, 4)
    to_smem.start()

    g[0] = jnp.transpose(f[0])
    for h in range(1, C):
        ft[h - 1] = jnp.transpose(jnp.concatenate([f[2 * h - 1], f[2 * h]], axis=1))
    for h in range(1, C):
        g[pl.ds(2 * h - 1, 2)] = mm(ft[h - 1], g[h - 1]).astype(BF16).reshape(2, R, R)

    get_cpart.wait()
    get_ccount.wait()
    for t in range(3):
        for j in range(2**t):
            i = 2**t - 1 + j
            for k in range(K):
                p = cpart_s[i, 0, k]
                its = lax.shift_right_logical(p, t)
                inside = p - lax.shift_left(its, t)
                place = lax.rem(its, NY) * NZ + lax.div(its, NY)
                here = jnp.logical_and(k < ccount_s[0, i], inside == lax.div(chip, 2 ** (2 - t)))
                cindex_s[i * K + k] = jnp.where(here, place + (2 - t) * LEAF, ZERO_P)
    get_cs.wait()
    for i in range(7):
        for k0 in range(0, K, 4):
            cscat[i, :, pl.ds(k0 * R, 4 * R)] = jnp.concatenate([cs[i, k] for k in range(k0, k0 + 4)], axis=1)

    for i in (0, 6, 1, 5, 2, 4, 3):
        over_z[i].wait_recv()
        for copy in over_y[i]:
            copy.start()
    get_su.start()

    for copy in halo_b:
        copy.wait_recv()
    to_smem.wait()
    for side in range(2):
        for i in range(C):
            xb[2 * C * side + i] = unfold(recv_b[side, i])
    for side, end in ((0, 0), (1, DEVICES - 1)):

        @pl.when(me == end)
        def _():
            xb[pl.ds(2 * C * side, C)] = jnp.zeros((C, R, R), BF16)

    get_sb.wait()

    @pl.loop(0, C, unroll=C)
    def _(i):
        zb[i] = couple(index_s, 0, UP + i, s, xb)

    def spread(y, z):
        at = y * NZ + z
        v = pool[y, z]
        xc[at] = v[:H, :R]
        xc[LEAF + at] = v[:H, R:]
        xc[2 * LEAF + at] = unfold(v[H:])

    for i in range(NZ):
        spread(at_y, lax.rem(at_z + i, NZ))
    for i in (7, 0, 6, 1, 5, 2, 4, 3):
        for copy in over_y[i]:
            copy.wait_recv()
        for m in range(1, NY):
            spread(lax.rem(at_y + m, NY), lax.rem(at_z + NZ - 1 - i, NZ))
    zc = []
    for i in range(7):
        left = jnp.concatenate([xc[cindex_s[i * K + k]] for k in range(K)], axis=1)
        zc.append(mm_nt(left, cscat[i]))
    y1 = jnp.concatenate([zc[1], zc[2]], axis=1) + mm(
        zc[0].astype(BF16), jnp.concatenate([cf[0], cf[1]], axis=1)
    )
    y1 = y1.astype(BF16)
    y2a = jnp.concatenate([zc[3], zc[4]], axis=1) + mm(y1[:, :R], jnp.concatenate([cf[2], cf[3]], axis=1))
    y2b = jnp.concatenate([zc[5], zc[6]], axis=1) + mm(y1[:, R:], jnp.concatenate([cf[4], cf[5]], axis=1))
    for j, v in enumerate((y2a, y2b)):
        ys[2 * j] = fold(v[:, :R])
        ys[2 * j + 1] = fold(v[:, R:])
    lows = [
        remote(ys.at[lax.div(peer, 2)], yr.at[sub], low_s.at[i], low_r.at[i], (leaf, peer))
        for i, peer in enumerate(group)
    ]
    for copy in lows:
        copy.start()
    yr[pl.ds(sub, 1)] = ys[pl.ds(lax.div(sub, 2), 1)]

    for copy in halo_u:
        copy.wait_recv()
    for side in range(2):
        for i in range(UP):
            xu[2 * UP * side + i] = unfold(recv_u[side, i])
    for side, end in ((0, 0), (1, DEVICES - 1)):

        @pl.when(me == end)
        def _():
            xu[pl.ds(2 * UP * side, UP)] = jnp.zeros((UP, R, R), BF16)

    get_su.wait()

    @pl.loop(0, UP, unroll=UP)
    def _(i):
        zu[i] = couple(index_s, 0, i, s, xu)

    w[0] = zu[0].astype(BF16)
    for h in range(1, C // 2):
        low = zu[pl.ds(2 * h - 1, 2)].reshape(2 * R, R) + mm(ft[h - 1], w[h - 1])
        w[pl.ds(2 * h - 1, 2)] = low.astype(BF16).reshape(2, R, R)

    for i in range(C // 2):
        h = C // 2 + i
        low = zb[pl.ds(2 * i, 2)].reshape(2 * R, R) + mm(ft[h - 1], w[h - 1])
        zb[pl.ds(2 * i, 2)] = low.reshape(2, R, R)

    for copy in lows:
        copy.wait_recv()
    halves = [unfold((yr[c] + yr[2 + c]) + (yr[4 + c] + yr[6 + c])) for c in range(2)]
    yp = jnp.concatenate(halves, axis=0).astype(BF16)
    far = mm_nt(g[pl.ds(UP, C)].reshape(C * R, R), yp).reshape(C, R, R)
    out[...] = (zb[...] + far).astype(BF16)
    for copy in [swap] + halo_b + halo_u + over_z + sum(over_y, []) + lows:
        copy.wait_send()


def on_device(
    bottom, transfer, coarse_transfer, coupling, partners, counts, coarse_coupling, coarse_partners, coarse_counts
):
    dma = pltpu.SemaphoreType.DMA
    any_space = pl.BlockSpec(memory_space=pltpu.HBM)
    return pl.pallas_call(
        kernel,
        out_shape=pltpu.VMEM((C, R, R), BF16),
        in_specs=[any_space] * 9,
        out_specs=pl.BlockSpec(memory_space=pltpu.VMEM),
        scratch_shapes=[
            pltpu.VMEM((3 * C + 1, R, R), BF16),
            pltpu.VMEM((3 * UP + 1, R, R), BF16),
            pltpu.VMEM((SLOTS, R, R), BF16),
            pltpu.VMEM((6, R, R), BF16),
            pltpu.VMEM((SLOTS, K, R, R), BF16),
            pltpu.VMEM((7, K, R, R), BF16),
            pltpu.VMEM((7, R, K * R), BF16),
            pltpu.VMEM((UP, 2 * R, R), BF16),
            pltpu.VMEM((SLOTS, R, R), BF16),
            pltpu.VMEM((UP, R, R), BF16),
            pltpu.VMEM((C, R, R), F32),
            pltpu.VMEM((UP, R, R), F32),
            pltpu.VMEM((C, R // 2, 2 * R), BF16),
            pltpu.VMEM((UP, R // 2, 2 * R), BF16),
            pltpu.VMEM((2, C, R // 2, 2 * R), BF16),
            pltpu.VMEM((2, UP, R // 2, 2 * R), BF16),
            pltpu.VMEM((2, H, R), F32),
            pltpu.VMEM((H, R), F32),
            pltpu.VMEM((3 * R, R), BF16),
            pltpu.VMEM((3 * H // 2, 2 * R), BF16),
            pltpu.VMEM((NY, NZ, 3 * H // 2, 2 * R), BF16),
            pltpu.VMEM((3 * LEAF + 1, H, R), BF16),
            pltpu.VMEM((4, H // 2, 2 * R), F32),
            pltpu.VMEM((SUB, H // 2, 2 * R), F32),
            pltpu.VMEM((K, SLOTS), jnp.int32),
            pltpu.VMEM((1, SLOTS), jnp.int32),
            pltpu.VMEM((K, 128), jnp.int32),
            pltpu.SMEM((K, 128), jnp.int32),
            pltpu.SMEM((7, 1, K), jnp.int32),
            pltpu.SMEM((1, 7), jnp.int32),
            pltpu.SMEM((7 * K,), jnp.int32),
            dma((7,)), dma((5,)),
            dma((4,)), dma((4,)), dma((1,)), dma((1,)), dma((7,)), dma((7,)),
            dma((NZ, NY - 1)), dma((NZ, NY - 1)), dma((7,)), dma((7,)),
        ],
        compiler_params=pltpu.CompilerParams(
            collective_id=0, has_side_effects=True, vmem_limit_bytes=64_800 * 2**10
        ),
        cost_estimate=pl.CostEstimate(flops=700_000_000, bytes_accessed=21_000_000, transcendentals=0),
    )(
        bottom,
        transfer.reshape(SLOTS, R, R),
        coarse_transfer.reshape(6, R, R),
        coupling.reshape(SLOTS, K, R, R),
        coarse_coupling.reshape(7, K, R, R),
        jnp.transpose(partners, (0, 2, 1)).reshape(K, SLOTS),
        counts,
        jnp.transpose(coarse_partners, (1, 0, 2)),
        coarse_counts,
    )


def solution(mesh):
    wide = P(("leaf", "sub"))
    placed = (wide, wide, P("leaf"), wide, wide, wide, P("leaf"), P("leaf"), P("leaf"))
    return jax.shard_map(on_device, mesh=mesh, in_specs=placed, out_specs=wide, check_vma=False)
```

```python
import jax
import jax.numpy as jnp
from jax import lax
from jax.experimental import pallas as pl
from jax.experimental.pallas import tpu as pltpu
from jax.sharding import PartitionSpec as P

F32 = jnp.float32
BF16 = jnp.bfloat16
MESH = pl.DeviceIdType.MESH

R = 64
K = 16
C = 32
UP = C - 1
SLOTS = 2 * C - 1
LEAF = 32
SUB = 8
NZ, NY = 8, 4
DEVICES = LEAF * SUB
ZERO_B = 3 * C
ZERO_U = 3 * UP
ZERO_P = 3 * LEAF
H = R // 2
NT = (((1,), (1,)), ((), ()))


def mm(a, b):
    return jnp.dot(a, b, preferred_element_type=F32)


def mm_nt(a, b):
    return lax.dot_general(a, b, NT, preferred_element_type=F32)


def fold(block):
    half = block.shape[0] // 2
    return jnp.concatenate([block[:half], block[half:]], axis=1)


def unfold(block):
    return jnp.concatenate([block[:, :R], block[:, R:]], axis=0)


def couple(index, first, slot, blocks, source):
    total = jnp.zeros((R, R), F32)
    for k0 in range(0, K, 4):
        left = jnp.concatenate([blocks[slot, k] for k in range(k0, k0 + 4)], axis=1)
        right = jnp.concatenate([source[index[k, slot]] for k in range(k0, k0 + 4)], axis=0)
        total = total + mm(left, right)
    return total


def kernel(
    bottom, transfer, coarse_transfer, coupling, coarse_coupling, partners, counts, coarse_partners, coarse_counts,
    out,
    xb, xu, f, cf, s, cs, cscat, ft, g, w, zb, zu,
    send_b, send_u, recv_b, recv_u, pt, pr, lift, mine, pool, xc, ys, yr,
    part_v, count_v, index_v, index_s, cpart_s, ccount_s, cindex_s,
    load_sem, small_sem, halo_s, halo_r, core_s, core_r, z_s, z_r, y_s, y_r, low_s, low_r,
):
    leaf = lax.axis_index("leaf")
    sub = lax.axis_index("sub")
    me = leaf * SUB + sub
    at_z = lax.div(leaf, NY)
    at_y = lax.rem(leaf, NY)
    chip = lax.div(sub, 2)
    core = lax.rem(sub, 2)
    after = lax.rem(me + 1, DEVICES)
    before = lax.rem(me + DEVICES - 1, DEVICES)
    sides = [(lax.div(d, SUB), lax.rem(d, SUB)) for d in (before, after)]
    group = [lax.rem(sub + i, SUB) for i in range(1, SUB)]
    along_z = [lax.rem(at_z + i, NZ) * NY + at_y for i in range(1, NZ)]
    along_y = [at_z * NY + lax.rem(at_y + i, NY) for i in range(1, NY)]

    load = lambda a, b, i: pltpu.make_async_copy(a, b, load_sem.at[i])
    get_x = load(bottom, xb.at[pl.ds(C, C)], 0)
    get_fb = load(transfer.at[pl.ds(UP, C)], f.at[pl.ds(UP, C)], 1)
    get_fu = load(transfer.at[pl.ds(0, UP)], f.at[pl.ds(0, UP)], 2)
    get_cf = load(coarse_transfer, cf, 3)
    get_cs = load(coarse_coupling, cs, 4)
    get_su = load(coupling.at[pl.ds(0, UP)], s.at[pl.ds(0, UP)], 5)
    get_sb = load(coupling.at[pl.ds(UP, C)], s.at[pl.ds(UP, C)], 6)
    small = lambda a, b, i: pltpu.make_async_copy(a, b, small_sem.at[i])
    get_part = small(partners, part_v, 0)
    get_count = small(counts, count_v, 1)
    get_cpart = small(coarse_partners, cpart_s, 2)
    get_ccount = small(coarse_counts, ccount_s, 3)
    for copy in (get_x, get_fb, get_fu, get_cf):
        copy.start()
    barrier = pltpu.get_barrier_semaphore()
    for peer in along_z + along_y:
        pl.semaphore_signal(barrier, inc=1, device_id=(peer, sub), device_id_type=MESH)
    for peer in sides:
        pl.semaphore_signal(barrier, inc=1, device_id=peer, device_id_type=MESH)
    for peer in group:
        pl.semaphore_signal(barrier, inc=1, device_id=(leaf, peer), device_id_type=MESH)

    for copy in (get_part, get_count, get_cpart, get_ccount):
        copy.start()
    xb[ZERO_B] = jnp.zeros((R, R), BF16)
    xu[ZERO_U] = jnp.zeros((R, R), BF16)
    xc[ZERO_P] = jnp.zeros((H, R), BF16)

    get_x.wait()
    get_fb.wait()
    get_fu.wait()
    n = C // 2
    while n >= 1:
        for i in range(n):
            a = 2 * (n + i) - 1
            left = jnp.concatenate([f[a], f[a + 1]], axis=1)
            right = (xb[pl.ds(C + 2 * i, 2)] if n == C // 2 else xu[pl.ds(UP + a, 2)]).reshape(2 * R, R)
            xu[UP + n + i - 1] = mm(left, right).astype(BF16)
        n //= 2
    pt[...] = jnp.transpose(mm(f[0], xu[UP])).reshape(2, H, R)

    pl.semaphore_wait(barrier, 2 + (SUB - 1) + (NZ - 1) + (NY - 1))

    def remote(src, dst, ss, rs, peer):
        return pltpu.make_async_remote_copy(
            src_ref=src, dst_ref=dst, send_sem=ss, recv_sem=rs, device_id=peer, device_id_type=MESH
        )

    swap = remote(pt.at[1 - core], pr, core_s.at[0], core_r.at[0], (leaf, chip * 2 + 1 - core))
    swap.start()
    get_cs.start()

    for i in range(C):
        send_b[i] = fold(xb[C + i])

    halo_b = [remote(send_b, recv_b.at[1 - i], halo_s.at[i], halo_r.at[i], sides[i]) for i in range(2)]
    halo_u = [remote(send_u, recv_u.at[1 - i], halo_s.at[2 + i], halo_r.at[2 + i], sides[i]) for i in range(2)]
    for copy in halo_b:
        copy.start()

    get_cf.wait()
    ones = lax.broadcasted_iota(jnp.int32, (R, R), 0) == lax.broadcasted_iota(jnp.int32, (R, R), 1)
    lift[pl.ds(0, R)] = ones.astype(F32).astype(BF16)
    lift[pl.ds(R, R)] = cf[2 + chip]
    lift[pl.ds(2 * R, R)] = mm(cf[lax.div(chip, 2)], cf[2 + chip]).astype(BF16)

    swap.wait_recv()
    node = (pt[pl.ds(core, 1)].reshape(H, R) + pr[...]).astype(BF16)
    piece = mm_nt(node, lift[...])
    mine[pl.ds(0, H)] = piece[:, : 2 * R].astype(BF16)
    mine[pl.ds(H, H // 2)] = fold(piece[:, 2 * R :]).astype(BF16)
    over_z = [
        remote(mine, pool.at[at_y, at_z], z_s.at[i], z_r.at[i], (peer, sub)) for i, peer in enumerate(along_z)
    ]
    over_y = [
        [
            remote(
                mine if i == NZ - 1 else pool.at[at_y, from_z],
                pool.at[at_y, from_z],
                y_s.at[i, m],
                y_r.at[i, m],
                (peer, sub),
            )
            for m, peer in ((1, along_y[1]), (0, along_y[0]), (2, along_y[2]))
        ]
        for i, from_z in enumerate([lax.rem(at_z + NZ - 1 - i, NZ) for i in range(NZ)])
    ]
    for i in (0, 6, 1, 5, 2, 4, 3):
        over_z[i].start()
    for copy in over_y[NZ - 1]:
        copy.start()
    get_sb.start()
    pool[pl.ds(at_y, 1), pl.ds(at_z, 1)] = mine[...].reshape(1, 1, 3 * H // 2, 2 * R)

    for i in range(UP):
        send_u[i] = fold(xu[UP + i])

    get_part.wait()
    get_count.wait()
    node = lax.broadcasted_iota(jnp.int32, (K, SLOTS), 1) + 1
    step = lax.broadcasted_iota(jnp.int32, (K, SLOTS), 0)
    width = jnp.ones((K, SLOTS), jnp.int32)
    for t in range(1, 6):
        width = jnp.where(node >= 2**t, 2**t, width)
    target = node - width + part_v[...]
    window = jnp.where(target < 0, 0, jnp.where(target < width, 1, 2))
    where_u = window * UP + (width - 1) + target + width - window * width
    is_bottom = node >= C
    where_from = jnp.where(is_bottom, C + target, where_u)
    ended = step >= jnp.broadcast_to(count_v[...], (K, SLOTS))
    where_from = jnp.where(ended, jnp.where(is_bottom, ZERO_B, ZERO_U), where_from)
    index_v[:, pl.ds(0, SLOTS)] = where_from
    to_smem = small(index_v, index_s, 4)
    to_smem.start()

    g[0] = jnp.transpose(f[0])
    for h in range(1, C):
        ft[h - 1] = jnp.transpose(jnp.concatenate([f[2 * h - 1], f[2 * h]], axis=1))
    for h in range(1, C):
        g[pl.ds(2 * h - 1, 2)] = mm(ft[h - 1], g[h - 1]).astype(BF16).reshape(2, R, R)

    get_cpart.wait()
    get_ccount.wait()
    for t in range(3):
        for j in range(2**t):
            i = 2**t - 1 + j
            for k in range(K):
                p = cpart_s[i, 0, k]
                its = lax.shift_right_logical(p, t)
                inside = p - lax.shift_left(its, t)
                place = lax.rem(its, NY) * NZ + lax.div(its, NY)
                here = jnp.logical_and(k < ccount_s[0, i], inside == lax.div(chip, 2 ** (2 - t)))
                cindex_s[i * K + k] = jnp.where(here, place + (2 - t) * LEAF, ZERO_P)
    get_cs.wait()
    for i in range(7):
        for k0 in range(0, K, 4):
            cscat[i, :, pl.ds(k0 * R, 4 * R)] = jnp.concatenate([cs[i, k] for k in range(k0, k0 + 4)], axis=1)

    for i in (0, 6, 1, 5, 2, 4, 3):
        over_z[i].wait_recv()
        for copy in over_y[i]:
            copy.start()
    for copy in halo_u:
        copy.start()
    get_su.start()

    for copy in halo_b:
        copy.wait_recv()
    to_smem.wait()
    for side in range(2):
        for i in range(C):
            xb[2 * C * side + i] = unfold(recv_b[side, i])
    for side, end in ((0, 0), (1, DEVICES - 1)):

        @pl.when(me == end)
        def _():
            xb[pl.ds(2 * C * side, C)] = jnp.zeros((C, R, R), BF16)

    get_sb.wait()

    @pl.loop(0, C, unroll=C)
    def _(i):
        zb[i] = couple(index_s, 0, UP + i, s, xb)

    def spread(y, z):
        at = y * NZ + z
        v = pool[y, z]
        xc[at] = v[:H, :R]
        xc[LEAF + at] = v[:H, R:]
        xc[2 * LEAF + at] = unfold(v[H:])

    for i in range(NZ):
        spread(at_y, lax.rem(at_z + i, NZ))
    for i in (7, 0, 6, 1, 5, 2, 4, 3):
        for copy in over_y[i]:
            copy.wait_recv()
        for m in range(1, NY):
            spread(lax.rem(at_y + m, NY), lax.rem(at_z + NZ - 1 - i, NZ))
    zc = []
    for i in range(7):
        left = jnp.concatenate([xc[cindex_s[i * K + k]] for k in range(K)], axis=1)
        zc.append(mm_nt(left, cscat[i]))
    y1 = jnp.concatenate([zc[1], zc[2]], axis=1) + mm(
        zc[0].astype(BF16), jnp.concatenate([cf[0], cf[1]], axis=1)
    )
    y1 = y1.astype(BF16)
    y2a = jnp.concatenate([zc[3], zc[4]], axis=1) + mm(y1[:, :R], jnp.concatenate([cf[2], cf[3]], axis=1))
    y2b = jnp.concatenate([zc[5], zc[6]], axis=1) + mm(y1[:, R:], jnp.concatenate([cf[4], cf[5]], axis=1))
    for j, v in enumerate((y2a, y2b)):
        v = v.astype(BF16)
        ys[2 * j] = fold(v[:, :R])
        ys[2 * j + 1] = fold(v[:, R:])
    lows = [
        remote(ys.at[lax.div(peer, 2)], yr.at[sub], low_s.at[i], low_r.at[i], (leaf, peer))
        for i, peer in enumerate(group)
    ]
    for copy in lows:
        copy.start()
    yr[pl.ds(sub, 1)] = ys[pl.ds(lax.div(sub, 2), 1)]

    for copy in halo_u:
        copy.wait_recv()
    for side in range(2):
        for i in range(UP):
            xu[2 * UP * side + i] = unfold(recv_u[side, i])
    for side, end in ((0, 0), (1, DEVICES - 1)):

        @pl.when(me == end)
        def _():
            xu[pl.ds(2 * UP * side, UP)] = jnp.zeros((UP, R, R), BF16)

    get_su.wait()

    @pl.loop(0, UP, unroll=UP)
    def _(i):
        zu[i] = couple(index_s, 0, i, s, xu)

    w[0] = zu[0].astype(BF16)
    for h in range(1, C // 2):
        low = zu[pl.ds(2 * h - 1, 2)].reshape(2 * R, R) + mm(ft[h - 1], w[h - 1])
        w[pl.ds(2 * h - 1, 2)] = low.astype(BF16).reshape(2, R, R)

    for i in range(C // 2):
        h = C // 2 + i
        low = zb[pl.ds(2 * i, 2)].reshape(2 * R, R) + mm(ft[h - 1], w[h - 1])
        zb[pl.ds(2 * i, 2)] = low.reshape(2, R, R)

    for copy in lows:
        copy.wait_recv()
    sent = yr[...].astype(F32)
    halves = [unfold((sent[c] + sent[2 + c]) + (sent[4 + c] + sent[6 + c])) for c in range(2)]
    yp = jnp.concatenate(halves, axis=0).astype(BF16)
    far = mm_nt(g[pl.ds(UP, C)].reshape(C * R, R), yp).reshape(C, R, R)
    out[...] = (zb[...] + far).astype(BF16)
    for copy in [swap] + halo_b + halo_u + over_z + sum(over_y, []) + lows:
        copy.wait_send()


def on_device(
    bottom, transfer, coarse_transfer, coupling, partners, counts, coarse_coupling, coarse_partners, coarse_counts
):
    dma = pltpu.SemaphoreType.DMA
    any_space = pl.BlockSpec(memory_space=pltpu.HBM)
    return pl.pallas_call(
        kernel,
        out_shape=pltpu.VMEM((C, R, R), BF16),
        in_specs=[any_space] * 9,
        out_specs=pl.BlockSpec(memory_space=pltpu.VMEM),
        scratch_shapes=[
            pltpu.VMEM((3 * C + 1, R, R), BF16),
            pltpu.VMEM((3 * UP + 1, R, R), BF16),
            pltpu.VMEM((SLOTS, R, R), BF16),
            pltpu.VMEM((6, R, R), BF16),
            pltpu.VMEM((SLOTS, K, R, R), BF16),
            pltpu.VMEM((7, K, R, R), BF16),
            pltpu.VMEM((7, R, K * R), BF16),
            pltpu.VMEM((UP, 2 * R, R), BF16),
            pltpu.VMEM((SLOTS, R, R), BF16),
            pltpu.VMEM((UP, R, R), BF16),
            pltpu.VMEM((C, R, R), F32),
            pltpu.VMEM((UP, R, R), F32),
            pltpu.VMEM((C, R // 2, 2 * R), BF16),
            pltpu.VMEM((UP, R // 2, 2 * R), BF16),
            pltpu.VMEM((2, C, R // 2, 2 * R), BF16),
            pltpu.VMEM((2, UP, R // 2, 2 * R), BF16),
            pltpu.VMEM((2, H, R), F32),
            pltpu.VMEM((H, R), F32),
            pltpu.VMEM((3 * R, R), BF16),
            pltpu.VMEM((3 * H // 2, 2 * R), BF16),
            pltpu.VMEM((NY, NZ, 3 * H // 2, 2 * R), BF16),
            pltpu.VMEM((3 * LEAF + 1, H, R), BF16),
            pltpu.VMEM((4, H // 2, 2 * R), BF16),
            pltpu.VMEM((SUB, H // 2, 2 * R), BF16),
            pltpu.VMEM((K, SLOTS), jnp.int32),
            pltpu.VMEM((1, SLOTS), jnp.int32),
            pltpu.VMEM((K, 128), jnp.int32),
            pltpu.SMEM((K, 128), jnp.int32),
            pltpu.SMEM((7, 1, K), jnp.int32),
            pltpu.SMEM((1, 7), jnp.int32),
            pltpu.SMEM((7 * K,), jnp.int32),
            dma((7,)), dma((5,)),
            dma((4,)), dma((4,)), dma((1,)), dma((1,)), dma((7,)), dma((7,)),
            dma((NZ, NY - 1)), dma((NZ, NY - 1)), dma((7,)), dma((7,)),
        ],
        compiler_params=pltpu.CompilerParams(
            collective_id=0, has_side_effects=True, vmem_limit_bytes=64_800 * 2**10
        ),
        cost_estimate=pl.CostEstimate(flops=700_000_000, bytes_accessed=21_000_000, transcendentals=0),
    )(
        bottom,
        transfer.reshape(SLOTS, R, R),
        coarse_transfer.reshape(6, R, R),
        coupling.reshape(SLOTS, K, R, R),
        coarse_coupling.reshape(7, K, R, R),
        jnp.transpose(partners, (0, 2, 1)).reshape(K, SLOTS),
        counts,
        jnp.transpose(coarse_partners, (1, 0, 2)),
        coarse_counts,
    )


def solution(mesh):
    wide = P(("leaf", "sub"))
    placed = (wide, wide, P("leaf"), wide, wide, wide, P("leaf"), P("leaf"), P("leaf"))
    return jax.shard_map(on_device, mesh=mesh, in_specs=placed, out_specs=wide, check_vma=False)
```

```python
import jax
import jax.numpy as jnp
from jax import lax
from jax.experimental import pallas as pl
from jax.experimental.pallas import tpu as pltpu
from jax.sharding import PartitionSpec as P

F32 = jnp.float32
BF16 = jnp.bfloat16
MESH = pl.DeviceIdType.MESH

R = 64
K = 16
C = 32
UP = C - 1
SLOTS = 2 * C - 1
LEAF = 32
SUB = 8
NZ, NY = 8, 4
DEVICES = LEAF * SUB
ZERO_B = 3 * C
ZERO_U = 3 * UP
ZERO_P = 3 * LEAF
H = R // 2
NT = (((1,), (1,)), ((), ()))


def mm(a, b):
    return jnp.dot(a, b, preferred_element_type=F32)


def mm_nt(a, b):
    return lax.dot_general(a, b, NT, preferred_element_type=F32)


def fold(block):
    half = block.shape[0] // 2
    return jnp.concatenate([block[:half], block[half:]], axis=1)


def unfold(block):
    return jnp.concatenate([block[:, :R], block[:, R:]], axis=0)


def couple(index, first, slot, blocks, source):
    total = jnp.zeros((R, R), F32)
    for k0 in range(0, K, 4):
        left = jnp.concatenate([blocks[slot, k] for k in range(k0, k0 + 4)], axis=1)
        right = jnp.concatenate([source[index[k, slot]] for k in range(k0, k0 + 4)], axis=0)
        total = total + mm(left, right)
    return total


def kernel(
    bottom, transfer, coarse_transfer, coupling, coarse_coupling, partners, counts, coarse_partners, coarse_counts,
    out,
    xb, xu, f, cf, s, cs, cscat, ft, g, w, zb, zu,
    send_b, send_u, recv_b, recv_u, pt, pr, lift, down, mine, pool, xc, ys, yr,
    part_v, count_v, index_v, index_s, cpart_s, ccount_s, cindex_s,
    load_sem, small_sem, halo_s, halo_r, core_s, core_r, z_s, z_r, y_s, y_r, low_s, low_r,
):
    leaf = lax.axis_index("leaf")
    sub = lax.axis_index("sub")
    me = leaf * SUB + sub
    at_z = lax.div(leaf, NY)
    at_y = lax.rem(leaf, NY)
    chip = lax.div(sub, 2)
    core = lax.rem(sub, 2)
    after = lax.rem(me + 1, DEVICES)
    before = lax.rem(me + DEVICES - 1, DEVICES)
    sides = [(lax.div(d, SUB), lax.rem(d, SUB)) for d in (before, after)]
    group = [lax.rem(sub + i, SUB) for i in range(1, SUB)]
    along_z = [lax.rem(at_z + i, NZ) * NY + at_y for i in range(1, NZ)]
    along_y = [at_z * NY + lax.rem(at_y + i, NY) for i in range(1, NY)]

    load = lambda a, b, i: pltpu.make_async_copy(a, b, load_sem.at[i])
    get_x = load(bottom, xb.at[pl.ds(C, C)], 0)
    get_fb = load(transfer.at[pl.ds(UP, C)], f.at[pl.ds(UP, C)], 1)
    get_fu = load(transfer.at[pl.ds(0, UP)], f.at[pl.ds(0, UP)], 2)
    get_cf = load(coarse_transfer, cf, 3)
    get_cs = load(coarse_coupling, cs, 4)
    get_su = load(coupling.at[pl.ds(0, UP)], s.at[pl.ds(0, UP)], 5)
    get_sb = load(coupling.at[pl.ds(UP, C)], s.at[pl.ds(UP, C)], 6)
    small = lambda a, b, i: pltpu.make_async_copy(a, b, small_sem.at[i])
    get_part = small(partners, part_v, 0)
    get_count = small(counts, count_v, 1)
    get_cpart = small(coarse_partners, cpart_s, 2)
    get_ccount = small(coarse_counts, ccount_s, 3)
    for copy in (get_x, get_fb, get_fu, get_cf):
        copy.start()
    barrier = pltpu.get_barrier_semaphore()
    for peer in along_z + along_y:
        pl.semaphore_signal(barrier, inc=1, device_id=(peer, sub), device_id_type=MESH)
    for peer in sides:
        pl.semaphore_signal(barrier, inc=1, device_id=peer, device_id_type=MESH)
    for peer in group:
        pl.semaphore_signal(barrier, inc=1, device_id=(leaf, peer), device_id_type=MESH)

    for copy in (get_part, get_count, get_cpart, get_ccount):
        copy.start()
    xb[ZERO_B] = jnp.zeros((R, R), BF16)
    xu[ZERO_U] = jnp.zeros((R, R), BF16)
    xc[ZERO_P] = jnp.zeros((H, R), BF16)

    get_x.wait()
    get_fb.wait()
    n = C // 2
    while n >= 1:
        if n == C // 4:
            get_fu.wait()
        for i in range(n):
            a = 2 * (n + i) - 1
            left = jnp.concatenate([f[a], f[a + 1]], axis=1)
            right = (xb[pl.ds(C + 2 * i, 2)] if n == C // 2 else xu[pl.ds(UP + a, 2)]).reshape(2 * R, R)
            xu[UP + n + i - 1] = mm(left, right).astype(BF16)
        n //= 2
    pt[...] = jnp.transpose(mm(f[0], xu[UP])).reshape(2, H, R)

    pl.semaphore_wait(barrier, 2 + (SUB - 1) + (NZ - 1) + (NY - 1))

    def remote(src, dst, ss, rs, peer):
        return pltpu.make_async_remote_copy(
            src_ref=src, dst_ref=dst, send_sem=ss, recv_sem=rs, device_id=peer, device_id_type=MESH
        )

    swap = remote(pt.at[1 - core], pr, core_s.at[0], core_r.at[0], (leaf, chip * 2 + 1 - core))
    swap.start()
    get_cs.start()

    for i in range(C):
        send_b[i] = fold(xb[C + i])

    halo_b = [remote(send_b, recv_b.at[1 - i], halo_s.at[i], halo_r.at[i], sides[i]) for i in range(2)]
    halo_u = [remote(send_u, recv_u.at[1 - i], halo_s.at[2 + i], halo_r.at[2 + i], sides[i]) for i in range(2)]
    for copy in halo_b:
        copy.start()

    get_cf.wait()
    ones = lax.broadcasted_iota(jnp.int32, (R, R), 0) == lax.broadcasted_iota(jnp.int32, (R, R), 1)
    lift[pl.ds(0, R)] = ones.astype(F32).astype(BF16)
    lift[pl.ds(R, R)] = cf[2 + chip]
    lift[pl.ds(2 * R, R)] = mm(cf[lax.div(chip, 2)], cf[2 + chip]).astype(BF16)

    swap.wait_recv()
    node = (pt[pl.ds(core, 1)].reshape(H, R) + pr[...]).astype(BF16)
    piece = mm_nt(node, lift[...])
    mine[pl.ds(0, H)] = piece[:, : 2 * R].astype(BF16)
    mine[pl.ds(H, H // 2)] = fold(piece[:, 2 * R :]).astype(BF16)
    over_z = [
        remote(mine, pool.at[at_y, at_z], z_s.at[i], z_r.at[i], (peer, sub)) for i, peer in enumerate(along_z)
    ]
    over_y = [
        [
            remote(
                mine if i == NZ - 1 else pool.at[at_y, from_z],
                pool.at[at_y, from_z],
                y_s.at[i, m],
                y_r.at[i, m],
                (peer, sub),
            )
            for m, peer in ((1, along_y[1]), (0, along_y[0]), (2, along_y[2]))
        ]
        for i, from_z in enumerate([lax.rem(at_z + NZ - 1 - i, NZ) for i in range(NZ)])
    ]
    for i in (0, 6, 1, 5, 2, 4, 3):
        over_z[i].start()
    for copy in over_y[NZ - 1]:
        copy.start()
    get_sb.start()
    pool[pl.ds(at_y, 1), pl.ds(at_z, 1)] = mine[...].reshape(1, 1, 3 * H // 2, 2 * R)

    for i in range(UP):
        send_u[i] = fold(xu[UP + i])

    get_part.wait()
    get_count.wait()
    node = lax.broadcasted_iota(jnp.int32, (K, SLOTS), 1) + 1
    step = lax.broadcasted_iota(jnp.int32, (K, SLOTS), 0)
    width = jnp.ones((K, SLOTS), jnp.int32)
    for t in range(1, 6):
        width = jnp.where(node >= 2**t, 2**t, width)
    target = node - width + part_v[...]
    window = jnp.where(target < 0, 0, jnp.where(target < width, 1, 2))
    where_u = window * UP + (width - 1) + target + width - window * width
    is_bottom = node >= C
    where_from = jnp.where(is_bottom, C + target, where_u)
    ended = step >= jnp.broadcast_to(count_v[...], (K, SLOTS))
    where_from = jnp.where(ended, jnp.where(is_bottom, ZERO_B, ZERO_U), where_from)
    index_v[:, pl.ds(0, SLOTS)] = where_from
    to_smem = small(index_v, index_s, 4)
    to_smem.start()

    blank = jnp.zeros((R, 2 * R), BF16)
    halves = [jnp.concatenate([cf[2 + 2 * j], cf[3 + 2 * j]], axis=1) for j in range(2)]
    down[pl.ds(0, R)] = jnp.concatenate([halves[0], blank], axis=1)
    down[pl.ds(R, R)] = jnp.concatenate([blank, halves[1]], axis=1)
    down[pl.ds(2 * R, R)] = jnp.concatenate([mm(cf[j], halves[j]).astype(BF16) for j in range(2)], axis=1)

    g[0] = jnp.transpose(f[0])
    for h in range(1, C):
        ft[h - 1] = jnp.transpose(jnp.concatenate([f[2 * h - 1], f[2 * h]], axis=1))
    for h in range(1, C):
        g[pl.ds(2 * h - 1, 2)] = mm(ft[h - 1], g[h - 1]).astype(BF16).reshape(2, R, R)

    get_cpart.wait()
    get_ccount.wait()
    for t in range(3):
        for j in range(2**t):
            i = 2**t - 1 + j
            for k in range(K):
                p = cpart_s[i, 0, k]
                its = lax.shift_right_logical(p, t)
                inside = p - lax.shift_left(its, t)
                place = lax.rem(its, NY) * NZ + lax.div(its, NY)
                here = jnp.logical_and(k < ccount_s[0, i], inside == lax.div(chip, 2 ** (2 - t)))
                cindex_s[i * K + k] = jnp.where(here, place + (2 - t) * LEAF, ZERO_P)
    get_cs.wait()
    for i in range(7):
        for k0 in range(0, K, 4):
            cscat[i, :, pl.ds(k0 * R, 4 * R)] = jnp.concatenate([cs[i, k] for k in range(k0, k0 + 4)], axis=1)

    for i in (0, 6, 1, 5, 2, 4, 3):
        over_z[i].wait_recv()
        for copy in over_y[i]:
            copy.start()
    for copy in halo_u:
        copy.start()
    get_su.start()

    for copy in halo_b:
        copy.wait_recv()
    to_smem.wait()
    for side in range(2):
        for i in range(C):
            xb[2 * C * side + i] = unfold(recv_b[side, i])
    for side, end in ((0, 0), (1, DEVICES - 1)):

        @pl.when(me == end)
        def _():
            xb[pl.ds(2 * C * side, C)] = jnp.zeros((C, R, R), BF16)

    get_sb.wait()

    @pl.loop(0, C, unroll=C)
    def _(i):
        zb[i] = couple(index_s, 0, UP + i, s, xb)

    def spread(y, z):
        at = y * NZ + z
        v = pool[y, z]
        xc[at] = v[:H, :R]
        xc[LEAF + at] = v[:H, R:]
        xc[2 * LEAF + at] = unfold(v[H:])

    for i in range(NZ):
        spread(at_y, lax.rem(at_z + i, NZ))
    for i in (7, 0, 6, 1, 5, 2, 4, 3):
        for copy in over_y[i]:
            copy.wait_recv()
        for m in range(1, NY):
            spread(lax.rem(at_y + m, NY), lax.rem(at_z + NZ - 1 - i, NZ))
    zc = []
    for i in range(7):
        left = jnp.concatenate([xc[cindex_s[i * K + k]] for k in range(K)], axis=1)
        zc.append(mm_nt(left, cscat[i]))
    upper = jnp.concatenate([zc[1], zc[2], zc[0]], axis=1).astype(BF16)
    y2 = jnp.concatenate(zc[3:], axis=1) + mm(upper, down[...])
    for j in range(2):
        v = y2[:, 2 * j * R : 2 * (j + 1) * R]
        v = v.astype(BF16)
        ys[2 * j] = fold(v[:, :R])
        ys[2 * j + 1] = fold(v[:, R:])
    lows = [
        remote(ys.at[lax.div(peer, 2)], yr.at[sub], low_s.at[i], low_r.at[i], (leaf, peer))
        for i, peer in enumerate(group)
    ]
    for copy in lows:
        copy.start()
    yr[pl.ds(sub, 1)] = ys[pl.ds(lax.div(sub, 2), 1)]

    for copy in halo_u:
        copy.wait_recv()
    for side in range(2):
        for i in range(UP):
            xu[2 * UP * side + i] = unfold(recv_u[side, i])
    for side, end in ((0, 0), (1, DEVICES - 1)):

        @pl.when(me == end)
        def _():
            xu[pl.ds(2 * UP * side, UP)] = jnp.zeros((UP, R, R), BF16)

    get_su.wait()

    @pl.loop(0, UP, unroll=UP)
    def _(i):
        zu[i] = couple(index_s, 0, i, s, xu)

    w[0] = zu[0].astype(BF16)
    for h in range(1, C // 2):
        low = zu[pl.ds(2 * h - 1, 2)].reshape(2 * R, R) + mm(ft[h - 1], w[h - 1])
        w[pl.ds(2 * h - 1, 2)] = low.astype(BF16).reshape(2, R, R)

    for i in range(C // 2):
        h = C // 2 + i
        low = zb[pl.ds(2 * i, 2)].reshape(2 * R, R) + mm(ft[h - 1], w[h - 1])
        zb[pl.ds(2 * i, 2)] = low.reshape(2, R, R)

    for copy in lows:
        copy.wait_recv()
    sent = yr[...].astype(F32)
    halves = [unfold((sent[c] + sent[2 + c]) + (sent[4 + c] + sent[6 + c])) for c in range(2)]
    yp = jnp.concatenate(halves, axis=0).astype(BF16)
    far = mm_nt(g[pl.ds(UP, C)].reshape(C * R, R), yp).reshape(C, R, R)
    out[...] = (zb[...] + far).astype(BF16)
    for copy in [swap] + halo_b + halo_u + over_z + sum(over_y, []) + lows:
        copy.wait_send()


def on_device(
    bottom, transfer, coarse_transfer, coupling, partners, counts, coarse_coupling, coarse_partners, coarse_counts
):
    dma = pltpu.SemaphoreType.DMA
    any_space = pl.BlockSpec(memory_space=pltpu.HBM)
    return pl.pallas_call(
        kernel,
        out_shape=pltpu.VMEM((C, R, R), BF16),
        in_specs=[any_space] * 9,
        out_specs=pl.BlockSpec(memory_space=pltpu.VMEM),
        scratch_shapes=[
            pltpu.VMEM((3 * C + 1, R, R), BF16),
            pltpu.VMEM((3 * UP + 1, R, R), BF16),
            pltpu.VMEM((SLOTS, R, R), BF16),
            pltpu.VMEM((6, R, R), BF16),
            pltpu.VMEM((SLOTS, K, R, R), BF16),
            pltpu.VMEM((7, K, R, R), BF16),
            pltpu.VMEM((7, R, K * R), BF16),
            pltpu.VMEM((UP, 2 * R, R), BF16),
            pltpu.VMEM((SLOTS, R, R), BF16),
            pltpu.VMEM((UP, R, R), BF16),
            pltpu.VMEM((C, R, R), F32),
            pltpu.VMEM((UP, R, R), F32),
            pltpu.VMEM((C, R // 2, 2 * R), BF16),
            pltpu.VMEM((UP, R // 2, 2 * R), BF16),
            pltpu.VMEM((2, C, R // 2, 2 * R), BF16),
            pltpu.VMEM((2, UP, R // 2, 2 * R), BF16),
            pltpu.VMEM((2, H, R), F32),
            pltpu.VMEM((H, R), F32),
            pltpu.VMEM((3 * R, R), BF16),
            pltpu.VMEM((3 * R, 4 * R), BF16),
            pltpu.VMEM((3 * H // 2, 2 * R), BF16),
            pltpu.VMEM((NY, NZ, 3 * H // 2, 2 * R), BF16),
            pltpu.VMEM((3 * LEAF + 1, H, R), BF16),
            pltpu.VMEM((4, H // 2, 2 * R), BF16),
            pltpu.VMEM((SUB, H // 2, 2 * R), BF16),
            pltpu.VMEM((K, SLOTS), jnp.int32),
            pltpu.VMEM((1, SLOTS), jnp.int32),
            pltpu.VMEM((K, 128), jnp.int32),
            pltpu.SMEM((K, 128), jnp.int32),
            pltpu.SMEM((7, 1, K), jnp.int32),
            pltpu.SMEM((1, 7), jnp.int32),
            pltpu.SMEM((7 * K,), jnp.int32),
            dma((7,)), dma((5,)),
            dma((4,)), dma((4,)), dma((1,)), dma((1,)), dma((7,)), dma((7,)),
            dma((NZ, NY - 1)), dma((NZ, NY - 1)), dma((7,)), dma((7,)),
        ],
        compiler_params=pltpu.CompilerParams(
            collective_id=0, has_side_effects=True, vmem_limit_bytes=64_800 * 2**10
        ),
        cost_estimate=pl.CostEstimate(flops=700_000_000, bytes_accessed=21_000_000, transcendentals=0),
    )(
        bottom,
        transfer.reshape(SLOTS, R, R),
        coarse_transfer.reshape(6, R, R),
        coupling.reshape(SLOTS, K, R, R),
        coarse_coupling.reshape(7, K, R, R),
        jnp.transpose(partners, (0, 2, 1)).reshape(K, SLOTS),
        counts,
        jnp.transpose(coarse_partners, (1, 0, 2)),
        coarse_counts,
    )


def solution(mesh):
    wide = P(("leaf", "sub"))
    placed = (wide, wide, P("leaf"), wide, wide, wide, P("leaf"), P("leaf"), P("leaf"))
    return jax.shard_map(on_device, mesh=mesh, in_specs=placed, out_specs=wide, check_vma=False)
```

```python
import jax
import jax.numpy as jnp
from jax import lax
from jax.experimental import pallas as pl
from jax.experimental.pallas import tpu as pltpu
from jax.sharding import PartitionSpec as P

F32 = jnp.float32
BF16 = jnp.bfloat16
MESH = pl.DeviceIdType.MESH

R = 64
K = 16
C = 32
UP = C - 1
SLOTS = 2 * C - 1
LEAF = 32
SUB = 8
NZ, NY = 8, 4
DEVICES = LEAF * SUB
ZERO_B = 3 * C
ZERO_U = 3 * UP
ZERO_P = 3 * LEAF
H = R // 2
NT = (((1,), (1,)), ((), ()))


def mm(a, b):
    return jnp.dot(a, b, preferred_element_type=F32)


def mm_nt(a, b):
    return lax.dot_general(a, b, NT, preferred_element_type=F32)


def fold(block):
    half = block.shape[0] // 2
    return jnp.concatenate([block[:half], block[half:]], axis=1)


def unfold(block):
    return jnp.concatenate([block[:, :R], block[:, R:]], axis=0)


def couple(index, first, slot, blocks, source):
    total = jnp.zeros((R, R), F32)
    for k0 in range(0, K, 4):
        left = jnp.concatenate([blocks[slot, k] for k in range(k0, k0 + 4)], axis=1)
        right = jnp.concatenate([source[index[k, slot]] for k in range(k0, k0 + 4)], axis=0)
        total = total + mm(left, right)
    return total


def kernel(
    bottom, transfer, coarse_transfer, coupling, coarse_coupling, partners, counts, coarse_partners, coarse_counts,
    out,
    xb, xu, f, cf, s, cs, cscat, ft, g, w, zb, zu,
    send_b, send_u, recv_b, recv_u, pt, pr, lift, down, mine, pool, xc, ys, yr,
    part_v, count_v, index_v, index_s, cpart_s, ccount_s, cindex_s,
    load_sem, small_sem, halo_s, halo_r, core_s, core_r, z_s, z_r, y_s, y_r, low_s, low_r,
):
    leaf = lax.axis_index("leaf")
    sub = lax.axis_index("sub")
    me = leaf * SUB + sub
    at_z = lax.div(leaf, NY)
    at_y = lax.rem(leaf, NY)
    chip = lax.div(sub, 2)
    core = lax.rem(sub, 2)
    after = lax.rem(me + 1, DEVICES)
    before = lax.rem(me + DEVICES - 1, DEVICES)
    sides = [(lax.div(d, SUB), lax.rem(d, SUB)) for d in (before, after)]
    group = [lax.rem(sub + i, SUB) for i in range(1, SUB)]
    along_z = [lax.rem(at_z + i, NZ) * NY + at_y for i in range(1, NZ)]
    along_y = [at_z * NY + lax.rem(at_y + i, NY) for i in range(1, NY)]

    load = lambda a, b, i: pltpu.make_async_copy(a, b, load_sem.at[i])
    get_x = load(bottom, xb.at[pl.ds(C, C)], 0)
    get_fb = load(transfer.at[pl.ds(UP, C)], f.at[pl.ds(UP, C)], 1)
    get_fu = load(transfer.at[pl.ds(0, UP)], f.at[pl.ds(0, UP)], 2)
    get_cf = load(coarse_transfer, cf, 3)
    get_cs = load(coarse_coupling, cs, 4)
    get_su = load(coupling.at[pl.ds(0, UP)], s.at[pl.ds(0, UP)], 5)
    get_sb = load(coupling.at[pl.ds(UP, C)], s.at[pl.ds(UP, C)], 6)
    small = lambda a, b, i: pltpu.make_async_copy(a, b, small_sem.at[i])
    get_part = small(partners, part_v, 0)
    get_count = small(counts, count_v, 1)
    get_cpart = small(coarse_partners, cpart_s, 2)
    get_ccount = small(coarse_counts, ccount_s, 3)
    for copy in (get_x, get_fb, get_fu, get_cf):
        copy.start()
    barrier = pltpu.get_barrier_semaphore()
    for peer in along_z + along_y:
        pl.semaphore_signal(barrier, inc=1, device_id=(peer, sub), device_id_type=MESH)
    for peer in sides:
        pl.semaphore_signal(barrier, inc=1, device_id=peer, device_id_type=MESH)
    for peer in group:
        pl.semaphore_signal(barrier, inc=1, device_id=(leaf, peer), device_id_type=MESH)

    for copy in (get_part, get_count, get_cpart, get_ccount):
        copy.start()
    xb[ZERO_B] = jnp.zeros((R, R), BF16)
    xu[ZERO_U] = jnp.zeros((R, R), BF16)
    xc[ZERO_P] = jnp.zeros((H, R), BF16)

    get_x.wait()
    get_fb.wait()
    n = C // 2
    while n >= 1:
        if n == C // 4:
            get_fu.wait()
        for i in range(n):
            a = 2 * (n + i) - 1
            left = jnp.concatenate([f[a], f[a + 1]], axis=1)
            right = (xb[pl.ds(C + 2 * i, 2)] if n == C // 2 else xu[pl.ds(UP + a, 2)]).reshape(2 * R, R)
            xu[UP + n + i - 1] = mm(left, right).astype(BF16)
        n //= 2
    pt[...] = jnp.transpose(mm(f[0], xu[UP])).reshape(2, H, R)

    pl.semaphore_wait(barrier, 2 + (SUB - 1) + (NZ - 1) + (NY - 1))

    def remote(src, dst, ss, rs, peer):
        return pltpu.make_async_remote_copy(
            src_ref=src, dst_ref=dst, send_sem=ss, recv_sem=rs, device_id=peer, device_id_type=MESH
        )

    swap = remote(pt.at[1 - core], pr, core_s.at[0], core_r.at[0], (leaf, chip * 2 + 1 - core))
    swap.start()
    get_cs.start()

    for i in range(UP):
        send_u[i] = fold(xu[UP + i])

    halo_b = [remote(send_b, recv_b.at[1 - i], halo_s.at[i], halo_r.at[i], sides[i]) for i in range(2)]
    halo_u = [remote(send_u, recv_u.at[1 - i], halo_s.at[2 + i], halo_r.at[2 + i], sides[i]) for i in range(2)]
    for copy, end in zip(halo_u, (0, DEVICES - 1)):

        @pl.when(me != end)
        def _():
            copy.start()


    get_cf.wait()
    ones = lax.broadcasted_iota(jnp.int32, (R, R), 0) == lax.broadcasted_iota(jnp.int32, (R, R), 1)
    lift[pl.ds(0, R)] = ones.astype(F32).astype(BF16)
    lift[pl.ds(R, R)] = cf[2 + chip]
    lift[pl.ds(2 * R, R)] = mm(cf[lax.div(chip, 2)], cf[2 + chip]).astype(BF16)

    swap.wait_recv()
    node = (pt[pl.ds(core, 1)].reshape(H, R) + pr[...]).astype(BF16)
    piece = mm_nt(node, lift[...])
    mine[pl.ds(0, H)] = piece[:, : 2 * R].astype(BF16)
    mine[pl.ds(H, H // 2)] = fold(piece[:, 2 * R :]).astype(BF16)
    over_z = [
        remote(mine, pool.at[at_y, at_z], z_s.at[i], z_r.at[i], (peer, sub)) for i, peer in enumerate(along_z)
    ]
    over_y = [
        [
            remote(
                mine if i == NZ - 1 else pool.at[at_y, from_z],
                pool.at[at_y, from_z],
                y_s.at[i, m],
                y_r.at[i, m],
                (peer, sub),
            )
            for m, peer in ((1, along_y[1]), (0, along_y[0]), (2, along_y[2]))
        ]
        for i, from_z in enumerate([lax.rem(at_z + NZ - 1 - i, NZ) for i in range(NZ)])
    ]
    for i in (0, 6, 1, 5, 2, 4, 3):
        over_z[i].start()
    for copy in over_y[NZ - 1]:
        copy.start()
    get_su.start()
    pool[pl.ds(at_y, 1), pl.ds(at_z, 1)] = mine[...].reshape(1, 1, 3 * H // 2, 2 * R)

    for i in range(C):
        send_b[i] = fold(xb[C + i])

    get_part.wait()
    get_count.wait()
    node = lax.broadcasted_iota(jnp.int32, (K, SLOTS), 1) + 1
    step = lax.broadcasted_iota(jnp.int32, (K, SLOTS), 0)
    width = jnp.ones((K, SLOTS), jnp.int32)
    for t in range(1, 6):
        width = jnp.where(node >= 2**t, 2**t, width)
    target = node - width + part_v[...]
    window = jnp.where(target < 0, 0, jnp.where(target < width, 1, 2))
    where_u = window * UP + (width - 1) + target + width - window * width
    is_bottom = node >= C
    where_from = jnp.where(is_bottom, C + target, where_u)
    ended = step >= jnp.broadcast_to(count_v[...], (K, SLOTS))
    where_from = jnp.where(ended, jnp.where(is_bottom, ZERO_B, ZERO_U), where_from)
    index_v[:, pl.ds(0, SLOTS)] = where_from
    to_smem = small(index_v, index_s, 4)
    to_smem.start()

    blank = jnp.zeros((R, 2 * R), BF16)
    halves = [jnp.concatenate([cf[2 + 2 * j], cf[3 + 2 * j]], axis=1) for j in range(2)]
    down[pl.ds(0, R)] = jnp.concatenate([halves[0], blank], axis=1)
    down[pl.ds(R, R)] = jnp.concatenate([blank, halves[1]], axis=1)
    down[pl.ds(2 * R, R)] = jnp.concatenate([mm(cf[j], halves[j]).astype(BF16) for j in range(2)], axis=1)

    g[0] = jnp.transpose(f[0])
    for h in range(1, C):
        ft[h - 1] = jnp.transpose(jnp.concatenate([f[2 * h - 1], f[2 * h]], axis=1))
    for h in range(1, C):
        g[pl.ds(2 * h - 1, 2)] = mm(ft[h - 1], g[h - 1]).astype(BF16).reshape(2, R, R)

    get_cpart.wait()
    get_ccount.wait()
    for t in range(3):
        for j in range(2**t):
            i = 2**t - 1 + j
            for k in range(K):
                p = cpart_s[i, 0, k]
                its = lax.shift_right_logical(p, t)
                inside = p - lax.shift_left(its, t)
                place = lax.rem(its, NY) * NZ + lax.div(its, NY)
                here = jnp.logical_and(k < ccount_s[0, i], inside == lax.div(chip, 2 ** (2 - t)))
                cindex_s[i * K + k] = jnp.where(here, place + (2 - t) * LEAF, ZERO_P)
    get_cs.wait()
    for i in range(7):
        for k0 in range(0, K, 4):
            cscat[i, :, pl.ds(k0 * R, 4 * R)] = jnp.concatenate([cs[i, k] for k in range(k0, k0 + 4)], axis=1)

    for i in (0, 6, 1, 5, 2, 4, 3):
        over_z[i].wait_recv()
        for copy in over_y[i]:
            copy.start()
    for copy, end in zip(halo_b, (0, DEVICES - 1)):

        @pl.when(me != end)
        def _():
            copy.start()

    get_sb.start()

    for copy, end in zip(halo_u, (DEVICES - 1, 0)):

        @pl.when(me != end)
        def _():
            copy.wait_recv()

    to_smem.wait()
    for side in range(2):
        for i in range(UP):
            xu[2 * UP * side + i] = unfold(recv_u[side, i])
    for side, end in ((0, 0), (1, DEVICES - 1)):

        @pl.when(me == end)
        def _():
            xu[pl.ds(2 * UP * side, UP)] = jnp.zeros((UP, R, R), BF16)

    get_su.wait()

    @pl.loop(0, UP, unroll=UP)
    def _(i):
        zu[i] = couple(index_s, 0, i, s, xu)

    w[0] = zu[0].astype(BF16)
    for h in range(1, C // 2):
        low = zu[pl.ds(2 * h - 1, 2)].reshape(2 * R, R) + mm(ft[h - 1], w[h - 1])
        w[pl.ds(2 * h - 1, 2)] = low.astype(BF16).reshape(2, R, R)

    def spread(y, z):
        at = y * NZ + z
        v = pool[y, z]
        xc[at] = v[:H, :R]
        xc[LEAF + at] = v[:H, R:]
        xc[2 * LEAF + at] = unfold(v[H:])

    for i in range(NZ):
        spread(at_y, lax.rem(at_z + i, NZ))
    for i in (7, 0, 6, 1, 5, 2, 4, 3):
        for copy in over_y[i]:
            copy.wait_recv()
        for m in range(1, NY):
            spread(lax.rem(at_y + m, NY), lax.rem(at_z + NZ - 1 - i, NZ))
    zc = []
    for i in range(7):
        left = jnp.concatenate([xc[cindex_s[i * K + k]] for k in range(K)], axis=1)
        zc.append(mm_nt(left, cscat[i]))
    upper = jnp.concatenate([zc[1], zc[2], zc[0]], axis=1).astype(BF16)
    y2 = jnp.concatenate(zc[3:], axis=1) + mm(upper, down[...])
    for j in range(2):
        v = y2[:, 2 * j * R : 2 * (j + 1) * R]
        v = v.astype(BF16)
        ys[2 * j] = fold(v[:, :R])
        ys[2 * j + 1] = fold(v[:, R:])
    lows = [
        remote(ys.at[lax.div(peer, 2)], yr.at[sub], low_s.at[i], low_r.at[i], (leaf, peer))
        for i, peer in enumerate(group)
    ]
    for copy in lows:
        copy.start()
    yr[pl.ds(sub, 1)] = ys[pl.ds(lax.div(sub, 2), 1)]

    for copy, end in zip(halo_b, (DEVICES - 1, 0)):

        @pl.when(me != end)
        def _():
            copy.wait_recv()

    for side in range(2):
        for i in range(C):
            xb[2 * C * side + i] = unfold(recv_b[side, i])
    for side, end in ((0, 0), (1, DEVICES - 1)):

        @pl.when(me == end)
        def _():
            xb[pl.ds(2 * C * side, C)] = jnp.zeros((C, R, R), BF16)

    get_sb.wait()

    @pl.loop(0, C, unroll=C)
    def _(i):
        zb[i] = couple(index_s, 0, UP + i, s, xb)

    for i in range(C // 2):
        h = C // 2 + i
        low = zb[pl.ds(2 * i, 2)].reshape(2 * R, R) + mm(ft[h - 1], w[h - 1])
        zb[pl.ds(2 * i, 2)] = low.reshape(2, R, R)

    for copy in lows:
        copy.wait_recv()
    sent = yr[...].astype(F32)
    halves = [unfold((sent[c] + sent[2 + c]) + (sent[4 + c] + sent[6 + c])) for c in range(2)]
    yp = jnp.concatenate(halves, axis=0).astype(BF16)
    far = mm_nt(g[pl.ds(UP, C)].reshape(C * R, R), yp).reshape(C, R, R)
    out[...] = (zb[...] + far).astype(BF16)
    for copy, end in zip(halo_b, (0, DEVICES - 1)):

        @pl.when(me != end)
        def _():
            copy.wait_send()

    for copy, end in zip(halo_u, (0, DEVICES - 1)):

        @pl.when(me != end)
        def _():
            copy.wait_send()

    for copy in [swap] + over_z + sum(over_y, []) + lows:
        copy.wait_send()


def on_device(
    bottom, transfer, coarse_transfer, coupling, partners, counts, coarse_coupling, coarse_partners, coarse_counts
):
    dma = pltpu.SemaphoreType.DMA
    any_space = pl.BlockSpec(memory_space=pltpu.HBM)
    return pl.pallas_call(
        kernel,
        out_shape=pltpu.VMEM((C, R, R), BF16),
        in_specs=[any_space] * 9,
        out_specs=pl.BlockSpec(memory_space=pltpu.VMEM),
        scratch_shapes=[
            pltpu.VMEM((3 * C + 1, R, R), BF16),
            pltpu.VMEM((3 * UP + 1, R, R), BF16),
            pltpu.VMEM((SLOTS, R, R), BF16),
            pltpu.VMEM((6, R, R), BF16),
            pltpu.VMEM((SLOTS, K, R, R), BF16),
            pltpu.VMEM((7, K, R, R), BF16),
            pltpu.VMEM((7, R, K * R), BF16),
            pltpu.VMEM((UP, 2 * R, R), BF16),
            pltpu.VMEM((SLOTS, R, R), BF16),
            pltpu.VMEM((UP, R, R), BF16),
            pltpu.VMEM((C, R, R), F32),
            pltpu.VMEM((UP, R, R), F32),
            pltpu.VMEM((C, R // 2, 2 * R), BF16),
            pltpu.VMEM((UP, R // 2, 2 * R), BF16),
            pltpu.VMEM((2, C, R // 2, 2 * R), BF16),
            pltpu.VMEM((2, UP, R // 2, 2 * R), BF16),
            pltpu.VMEM((2, H, R), F32),
            pltpu.VMEM((H, R), F32),
            pltpu.VMEM((3 * R, R), BF16),
            pltpu.VMEM((3 * R, 4 * R), BF16),
            pltpu.VMEM((3 * H // 2, 2 * R), BF16),
            pltpu.VMEM((NY, NZ, 3 * H // 2, 2 * R), BF16),
            pltpu.VMEM((3 * LEAF + 1, H, R), BF16),
            pltpu.VMEM((4, H // 2, 2 * R), BF16),
            pltpu.VMEM((SUB, H // 2, 2 * R), BF16),
            pltpu.VMEM((K, SLOTS), jnp.int32),
            pltpu.VMEM((1, SLOTS), jnp.int32),
            pltpu.VMEM((K, 128), jnp.int32),
            pltpu.SMEM((K, 128), jnp.int32),
            pltpu.SMEM((7, 1, K), jnp.int32),
            pltpu.SMEM((1, 7), jnp.int32),
            pltpu.SMEM((7 * K,), jnp.int32),
            dma((7,)), dma((5,)),
            dma((4,)), dma((4,)), dma((1,)), dma((1,)), dma((7,)), dma((7,)),
            dma((NZ, NY - 1)), dma((NZ, NY - 1)), dma((7,)), dma((7,)),
        ],
        compiler_params=pltpu.CompilerParams(
            collective_id=0, has_side_effects=True, vmem_limit_bytes=64_800 * 2**10
        ),
        cost_estimate=pl.CostEstimate(flops=700_000_000, bytes_accessed=21_000_000, transcendentals=0),
    )(
        bottom,
        transfer.reshape(SLOTS, R, R),
        coarse_transfer.reshape(6, R, R),
        coupling.reshape(SLOTS, K, R, R),
        coarse_coupling.reshape(7, K, R, R),
        jnp.transpose(partners, (0, 2, 1)).reshape(K, SLOTS),
        counts,
        jnp.transpose(coarse_partners, (1, 0, 2)),
        coarse_counts,
    )


def solution(mesh):
    wide = P(("leaf", "sub"))
    placed = (wide, wide, P("leaf"), wide, wide, wide, P("leaf"), P("leaf"), P("leaf"))
    return jax.shard_map(on_device, mesh=mesh, in_specs=placed, out_specs=wide, check_vma=False)
```
